32 devices in a mesh: section: 2 (over core), seq: 4 (over z), head: 4 (over y, x).
Axes of the slice: x: 2, y: 2, z: 4, core: 2. Of those that a mesh axis runs over, the one named last changes fastest.
Arguments:
- query_vectors: bfloat16 [2, 512, 8192], P('section', 'seq', 'head'), may hold values from -400 to 400
- key_vectors: bfloat16 [2, 512, 8192], P('section', 'seq', 'head'), may hold values from -6 to 6
- value_vectors: bfloat16 [2, 512, 8192], P('section', 'seq', 'head'), may hold values from -6 to 6
- prior_state: float32 [2, 64, 128, 128], P('section', 'head'), may hold values from -64 to 64
- doc_ids: int32 [2, 512], P('section', 'seq'), may hold values from 0 to 3, never falling along the last dimension, each value on 1 to 256 neighbouring positions
- norm_gain: float32 [2, 8192], P('section', 'head'), may hold values from 0.25 to 1.75
- residual: bfloat16 [2, 512, 6144], P('section', 'head', 'seq'), may hold values from -6 to 6
- out_weight: bfloat16 [2, 8192, 6144], P('section', 'head', 'seq'), may hold values from -0.0625 to 0.0625
- enc_weight: bfloat16 [2, 6144, 32768], P('section', None, ('seq', 'head')), may hold values from -0.078125 to 0.078125
- enc_bias: float32 [2, 32768], P('section', ('seq', 'head')), may hold values from -5 to 5
Outputs:
- handoff: bfloat16 [2, 512, 6144], P('section', 'head', 'seq')
- monitor: bfloat16 [2, 8, 32768], P('section', None, ('seq', 'head'))
The draws below stay inside these ranges and needn't reach their ends.
Inputs may be any that keep to these rules, and one draw needn't show every extreme that they name: `doc_ids`: document numbers never fall along a section's tokens, are 0 at its first token and rise by at most 1 from one token to the next; a document has at most 256 tokens, and one has exactly that many.
All inputs are finite; a program needn't handle non-finite values.
Results may differ from the reference program's by a relative error of at most 0.0039.
Values may be sent and summed in bfloat16 or wider, within the bound.
A program may use at most 128 MiB of HBM per device.

```python
import math
import jax
import jax.numpy as jnp
import numpy as np
from jax import lax

D = 6144
HEADS = 64
HD = 128
LAT = 32768
POOL = 64
TOK_DEV = 128
SECTIONS = 2
TOKENS = 512
HDIM = 8192


def draw_query_vectors(key, part):
    first_key, second_key = jax.random.split(key)
    full_shape = (SECTIONS, TOKENS, HEADS * HD)
    head_number = (jnp.arange(HEADS * HD) // HD).astype(jnp.float32)
    raw_values = jnp.clip(jax.random.normal(first_key, full_shape, jnp.float32), -4.0, 4.0)
    head_scale = jnp.exp(head_number * (math.log(10.0) / HEADS))
    row_scale = jnp.exp(jax.random.uniform(second_key, (SECTIONS, TOKENS, 1), jnp.float32) * math.log(10.0))
    return (raw_values * row_scale * head_scale).astype(jnp.bfloat16)


def steps_of(key, extent, shards, smallest, largest):
    level, own = 1.0, jax.random.fold_in(key, 6)
    for position, blocks in shards:
        heights = jnp.exp(jax.random.uniform(jax.random.fold_in(own, position), (blocks,), jnp.float32, smallest / len(shards), largest / len(shards)))
        level = level * jnp.repeat(heights, extent[position] // blocks).reshape([-1 if axis == position else 1 for axis in range(len(extent))])
    return level


def length_profile(number_of, total, bound, lean):
    weights = [(1 << 20) // math.isqrt(grade ** lean) + 1 for grade in range(2, number_of + 1)]
    rest, counts = total - bound - (number_of - 1), [1] * (number_of - 1)
    while rest > 0:
        candidates = [i for i in range(number_of - 1) if counts[i] < bound]
        pool, left = sum([weights[i] for i in candidates]), rest
        for i in candidates:
            extra = min(bound - counts[i], max(1, left * weights[i] // pool), rest)
            counts[i] = counts[i] + extra
            rest = rest - extra
    return np.array([bound] + counts)


def uneven_parts(own_key, count, total, limit, slope):
    if count == 2:
        one = jax.random.randint(own_key, (), max(1, total - limit), min(limit, total - 1) + 1)
        return jnp.stack([one, total - one])
    tallies = jnp.asarray(length_profile(count, total, limit, slope), jnp.int32)
    twos = (count - 1) // 2
    donor, taker = tallies[1:1 + 2 * twos:2], tallies[2:2 + 2 * twos:2]
    margin = jnp.minimum(donor - 1, limit - taker)
    passed = jax.random.randint(jax.random.fold_in(own_key, 1), (twos,), 0, 1 << 20) % (margin + 1)
    tallies = tallies.at[1:1 + 2 * twos:2].set(donor - passed).at[2:2 + 2 * twos:2].set(taker + passed)
    return tallies[jax.random.permutation(jax.random.fold_in(own_key, 2), count)]


def scatter_about(key, extent, width, limit, cuts=(), held_as=jnp.bfloat16):
    values = width * jax.random.normal(key, extent, jnp.float32)
    if cuts:
        values = values * steps_of(key, extent, cuts, -0.22, 0.18)
    return jnp.clip(values, -limit, limit).astype(held_as)


def setup_inputs(seed: int = 0) -> dict:
    key_list = jax.random.split(jax.random.key(seed), 11)
    query_vectors = draw_query_vectors(jax.random.fold_in(key_list[10], 71), 0)
    key_vectors = scatter_about(key_list[1], (SECTIONS, TOKENS, HDIM), 1.0, 6.0, ((0, 2), (1, 4), (2, 4)))
    value_vectors = scatter_about(key_list[2], (SECTIONS, TOKENS, HDIM), 1.0, 6.0, ((0, 2), (1, 4), (2, 4)))
    prior_state = scatter_about(key_list[3], (SECTIONS, HEADS, HD, HD), ((TOKENS // 4) ** 0.5), 64.0, ((0, 2), (1, 4)), jnp.float32)
    doc_ids = jax.vmap(lambda own: jnp.searchsorted(jnp.cumsum(uneven_parts(own, 4, TOKENS, TOKENS // 2, 0)), jnp.arange(TOKENS), side="right"))(jax.random.split(key_list[4], SECTIONS)).reshape((SECTIONS, TOKENS)).astype(jnp.int32)
    norm_gain = jnp.clip(1.0 + 0.15 * jax.random.normal(key_list[5], (SECTIONS, HDIM), jnp.float32), 0.25, 1.75)
    residual = scatter_about(key_list[6], (SECTIONS, TOKENS, D), 1.0, 6.0, ((0, 2), (1, 4), (2, 4)))
    out_weight = scatter_about(key_list[7], (SECTIONS, HDIM, D), HDIM ** -0.5, 0.0625, ((0, 2), (1, 4), (2, 4)))
    enc_weight = scatter_about(key_list[8], (SECTIONS, D, LAT), D ** -0.5, 0.078125, ((0, 2), (2, 16)))
    enc_bias = scatter_about(key_list[9], (SECTIONS, LAT), 1.0, 5.0, ((0, 2), (1, 16)), jnp.float32)
    return {"query_vectors": query_vectors, "key_vectors": key_vectors, "value_vectors": value_vectors, "prior_state": prior_state, "doc_ids": doc_ids, "norm_gain": norm_gain, "residual": residual, "out_weight": out_weight, "enc_weight": enc_weight, "enc_bias": enc_bias}


epsilon = 1e-06

def merge_states(first_pair, second_pair):
    first_state, first_doc = first_pair
    second_state, second_doc = second_pair
    top_doc = jnp.maximum(first_doc, second_doc)
    merged = jnp.where(first_doc == top_doc, first_state, 0.0) + jnp.where(second_doc == top_doc, second_state, 0.0)
    return (merged, top_doc)

def attend_section(query_rows, key_rows, value_rows, prior, doc_index):
    blocks = TOKENS // TOK_DEV
    highest = lax.Precision.HIGHEST

    def shaped(array):
        return array.reshape(blocks, TOK_DEV, HEADS, HD).astype(jnp.float32)
    doc_float = doc_index.astype(jnp.float32).reshape(blocks, TOK_DEV)
    positions = jnp.arange(TOK_DEV)
    causal = positions[None, :] <= positions[:, None]

    def advance(carried, block_data):
        state, last_doc = carried
        queries_f, keys_f, values_f, docs = block_data
        inter = jnp.einsum('thd,hde->the', queries_f, state, precision=highest)
        inter = inter * (docs == last_doc).astype(jnp.float32)[:, None, None]
        scores = jnp.einsum('thd,uhd->htu', queries_f, keys_f, precision=highest)
        same_doc = causal & (docs[:, None] == docs[None, :])
        scores = jnp.where(same_doc[None, :, :], scores, 0.0)
        intra = jnp.einsum('htu,uhe->the', scores, values_f, precision=highest)
        block_last = docs[-1]
        selected = jnp.where((docs == block_last)[:, None, None], keys_f, 0.0)
        summary = jnp.einsum('thd,the->hde', selected, values_f, precision=highest)
        return (merge_states((state, last_doc), (summary, block_last)), inter + intra)
    initial = (prior.astype(jnp.float32), jnp.zeros((), jnp.float32))
    _, outputs = lax.scan(advance, initial, (shaped(query_rows), shaped(key_rows), shaped(value_rows), doc_float))
    return outputs.reshape(TOKENS, HEADS * HD)

def reference(query_vectors, key_vectors, value_vectors, prior_state, doc_ids, norm_gain, residual, out_weight, enc_weight, enc_bias):
    handoffs = []
    monitors = []
    for section_index in range(SECTIONS):
        attended = attend_section(query_vectors[section_index], key_vectors[section_index], value_vectors[section_index], prior_state[section_index], doc_ids[section_index])
        mean_square = lax.optimization_barrier(jnp.mean(attended * attended, axis=1, keepdims=True))
        normed = (attended * lax.rsqrt(mean_square + epsilon) * norm_gain[section_index]).astype(jnp.bfloat16)
        projected = jnp.dot(normed, out_weight[section_index], preferred_element_type=jnp.float32)
        layer_out = (residual[section_index].astype(jnp.float32) + projected).astype(jnp.bfloat16)
        latent = jax.nn.relu(jnp.dot(layer_out, enc_weight[section_index], preferred_element_type=jnp.float32) + enc_bias[section_index])
        pooled = lax.optimization_barrier(jnp.mean(latent.reshape(TOKENS // POOL, POOL, LAT), axis=1)).astype(jnp.bfloat16)
        handoffs.append(layer_out)
        monitors.append(pooled)
    handoff = jnp.roll(jnp.stack(handoffs), 1, axis=0)
    monitor = jnp.roll(jnp.stack(monitors), 1, axis=0)
    return (handoff, monitor)
```

```python
import jax
import jax.numpy as jnp
from jax import lax
from jax.experimental import pallas as pl
from jax.experimental.pallas import tpu as pltpu
from jax.sharding import PartitionSpec as P

HD = 128
POOL = 64
HDIM = 8192


epsilon = 1e-06


def entering(part, axis, combine, identity):
    place = lax.axis_index(axis)
    gathered = jax.tree.map(lambda a: lax.all_gather(a, axis), part)
    state = jax.tree.map(lambda a, e: jnp.zeros_like(a) + jnp.asarray(e, a.dtype), part, identity)

    def one(hop, state):
        return combine(
            state, jax.tree.map(lambda a: lax.dynamic_index_in_dim(a, hop, 0, False), gathered)
        )

    return lax.fori_loop(0, place, one, state)


def passed_along(x, axis, by):
    devices = lax.axis_size(axis)
    return lax.ppermute(x, axis, [(i, (i + by) % devices) for i in range(devices)])


def merge_states(first_pair, second_pair):
    first_state, first_doc = first_pair
    second_state, second_doc = second_pair
    top_doc = jnp.maximum(first_doc, second_doc)
    merged = jnp.where(first_doc == top_doc, first_state, 0.0) + jnp.where(
        second_doc == top_doc, second_state, 0.0
    )
    return (merged, top_doc)


def local(
    query_vectors,
    key_vectors,
    value_vectors,
    prior_state,
    doc_ids,
    norm_gain,
    residual,
    out_weight,
    enc_weight,
    enc_bias,
):
    highest = lax.Precision.HIGHEST
    row_count = query_vectors.shape[1]
    local_heads = query_vectors.shape[2] // HD
    queries = query_vectors[0].reshape(row_count, local_heads, HD)
    keys_block = key_vectors[0].reshape(row_count, local_heads, HD)
    values_block = value_vectors[0].reshape(row_count, local_heads, HD)
    doc_index = doc_ids[0]
    doc_float = doc_index.astype(jnp.float32)
    last_doc = doc_float[-1]
    keys_last = jnp.where(
        (doc_index == doc_index[-1])[:, None, None], keys_block, jnp.zeros_like(keys_block)
    )
    summary = jnp.einsum(
        "thd,the->hde", keys_last, values_block, preferred_element_type=jnp.float32
    )
    identity_pair = (jnp.zeros_like(summary), jnp.full((1,), -1.0, jnp.float32))
    earlier_state, earlier_last = entering(
        (summary, last_doc[None]), "seq", merge_states, identity_pair
    )
    earlier_doc = earlier_last[0]
    incoming_state, incoming_doc = merge_states(
        (prior_state[0], jnp.zeros((), jnp.float32)), (earlier_state, earlier_doc)
    )
    inter = jnp.einsum(
        "thd,hde->the", queries.astype(jnp.float32), incoming_state, precision=highest
    )
    inter = inter * (doc_float == incoming_doc).astype(jnp.float32)[:, None, None]
    scores = jnp.einsum("thd,uhd->htu", queries, keys_block, preferred_element_type=jnp.float32)
    positions = jnp.arange(row_count)
    same_doc = (positions[None, :] <= positions[:, None]) & (
        doc_index[:, None] == doc_index[None, :]
    )
    scores = jnp.where(same_doc[None, :, :], scores, 0.0)
    intra = jnp.einsum("htu,uhe->the", scores, values_block.astype(jnp.float32), precision=highest)
    attended = (inter + intra).reshape(row_count, local_heads * HD)
    total_square = lax.psum(jnp.sum(attended * attended, axis=1), "head")
    inverse_rms = lax.rsqrt(total_square / HDIM + epsilon)
    normed = (attended * inverse_rms[:, None] * norm_gain[0]).astype(jnp.bfloat16)
    projection = out_weight[0]
    partial_sums = jnp.dot(
        lax.all_gather(normed, "seq", axis=0, tiled=True),
        projection,
        preferred_element_type=jnp.float32,
    )
    own_rows = residual[0]
    encoder = enc_weight[0]
    latent_width = encoder.shape[1]
    reduced = lax.psum_scatter(partial_sums, "head", scatter_dimension=0, tiled=True)
    layer_out = (own_rows.astype(jnp.float32) + reduced).astype(jnp.bfloat16)
    features = lax.all_gather(layer_out, "head", axis=0, tiled=True)
    pre_scores = jnp.dot(
        lax.all_gather(features, "seq", axis=1, tiled=True),
        encoder,
        preferred_element_type=jnp.float32,
    )
    latent = jax.nn.relu(pre_scores + enc_bias[0])
    pooled = jnp.mean(latent.reshape(-1, POOL, latent_width), axis=1).astype(jnp.bfloat16)
    handoff, monitor = passed_along((layer_out[None], pooled[None]), "section", 1)
    return (handoff, monitor)


MESH = pl.DeviceIdType.MESH
F32 = jnp.float32
BF16 = jnp.bfloat16
SEQ = 4
GROUP = 4
HALVES = 2
HEAD_CHUNKS = 4


def fused_kernel(
    q_ref,
    k_ref,
    v_ref,
    prior_ref,
    doc_ref,
    gain_ref,
    res_ref,
    ow_hbm,
    enc_hbm,
    bias_ref,
    hand_ref,
    mon_ref,
    ow,
    enc,
    doc_own,
    doc_prev,
    state_in,
    state_out,
    summary,
    attended,
    sq_own,
    sq_in,
    rows,
    part,
    part_out,
    part_in,
    feats,
    hand_in,
    acc,
    pool,
    pool_in,
    ow_sem,
    enc_sem,
    doc_sem,
    st_s,
    st_r,
    sq_s,
    sq_r,
    row_s,
    row_r,
    part_s,
    part_r,
    zg_s,
    zg_r,
    x_s,
    x_r,
    y_s,
    y_r,
    d_s,
    d_r,
    hand_s,
    hand_r,
    pool_sem,
):
    s = lax.axis_index("section")
    z = lax.axis_index("seq")
    h = lax.axis_index("head")
    tokens = q_ref.shape[1]
    half = tokens // HALVES
    heads = q_ref.shape[2] // HD
    per_chunk = heads // HEAD_CHUNKS
    width = res_ref.shape[2]
    latents = bias_ref.shape[1]
    x_peer = h + 1 - 2 * lax.rem(h, 2)
    y_peer = lax.rem(h + 2, 4)
    d_peer = 3 - h
    mates = (x_peer, y_peer, d_peer)

    def at(seq=None, head=None, section=None):
        return (
            s if section is None else section,
            z if seq is None else seq,
            h if head is None else head,
        )

    def remote(src, dst, send, recv, device):
        return pltpu.make_async_remote_copy(
            src_ref=src, dst_ref=dst, send_sem=send, recv_sem=recv,
            device_id=device, device_id_type=MESH,
        )

    ow_copy = pltpu.make_async_copy(ow_hbm.at[0], ow, ow_sem)
    enc_copy = pltpu.make_async_copy(enc_hbm.at[0], enc, enc_sem)
    ow_copy.start()
    enc_copy.start()

    barrier = pltpu.get_barrier_semaphore()
    for k in range(1, SEQ):
        pl.semaphore_signal(barrier, inc=1, device_id=at(seq=lax.rem(z + k, SEQ)), device_id_type=MESH)
    for mate in mates:
        pl.semaphore_signal(barrier, inc=1, device_id=at(head=mate), device_id_type=MESH)
    pl.semaphore_signal(barrier, inc=1, device_id=at(section=1 - s), device_id_type=MESH)
    pl.semaphore_wait(barrier, SEQ - 1 + 3 + 1)

    row_iota = lax.broadcasted_iota(jnp.int32, (tokens, tokens), 0)
    col_iota = lax.broadcasted_iota(jnp.int32, (tokens, tokens), 1)
    eye = row_iota == col_iota
    doc_own[...] = jnp.broadcast_to(doc_ref[...].astype(F32), doc_own.shape)
    later = jnp.minimum(z + 1, SEQ - 1)

    def doc_copy():
        return remote(doc_own, doc_prev, doc_sem.at[0], doc_sem.at[1], at(seq=later))

    def state_copy(c):
        return remote(state_out.at[c], state_in.at[c], st_s.at[c], st_r.at[c], at(seq=later))

    @pl.when(z < SEQ - 1)
    def _():
        doc_copy().start()

    doc_row = doc_own[0:1, :]
    doc_col = jnp.sum(jnp.where(eye, doc_row, 0.0), axis=1, keepdims=True)
    last_doc = jnp.max(doc_row, axis=1, keepdims=True)
    keep_key = doc_col == last_doc
    same_doc = (doc_col == doc_row) & (col_iota <= row_iota)

    def columns(head):
        return pl.ds(pl.multiple_of(head * HD, HD), HD)

    def summarize(head, carry):
        keys = k_ref[0, :, columns(head)]
        keys = jnp.where(keep_key, keys.astype(F32), 0.0).astype(BF16)
        summary[head] = lax.dot_general(
            keys, v_ref[0, :, columns(head)], (((0,), (0,)), ((), ())), preferred_element_type=F32
        )
        return carry

    def within(head, carry):
        cols = columns(head)
        values = v_ref[0, :, cols]
        scores = lax.dot_general(
            q_ref[0, :, cols], k_ref[0, :, cols], (((1,), (1,)), ((), ())), preferred_element_type=F32
        )
        scores = jnp.where(same_doc, scores, 0.0)
        high = scores.astype(BF16)
        low = (scores - high.astype(F32)).astype(BF16)
        attended[:, cols] = jnp.dot(high, values, preferred_element_type=F32) + jnp.dot(
            low, values, preferred_element_type=F32
        )
        return carry

    lax.fori_loop(0, heads, summarize, 0)

    @pl.when(z == 0)
    def _():
        doc_prev[...] = jnp.zeros_like(doc_prev)

    @pl.when(z > 0)
    def _():
        doc_copy().wait_recv()

    entering_doc = jnp.max(doc_prev[0:1, :], axis=1, keepdims=True)
    carried = jnp.where(last_doc == entering_doc, 1.0, 0.0)
    from_before = jnp.where(doc_col == entering_doc, 1.0, 0.0)

    squares = jnp.zeros((tokens, HD), F32)
    for c in range(HEAD_CHUNKS):
        first = c * per_chunk

        @pl.when(z == 0)
        def _():
            state_in[c] = prior_ref[0, first : first + per_chunk].astype(BF16)

        if c > 0:
            lax.fori_loop(first, first + per_chunk, within, 0)

        @pl.when(z > 0)
        def _():
            state_copy(c).wait_recv()

        @pl.when(z < SEQ - 1)
        def _():
            for i in range(per_chunk):
                state_out[c, i] = (state_in[c, i].astype(F32) * carried + summary[first + i]).astype(BF16)
            state_copy(c).start()

        if c == 0:
            lax.fori_loop(first, first + per_chunk, within, 0)

        for i in range(per_chunk):
            cols = slice((first + i) * HD, (first + i + 1) * HD)
            inter = jnp.dot(q_ref[0, :, cols], state_in[c, i], preferred_element_type=F32)
            total = attended[:, cols] + inter * from_before
            attended[:, cols] = total
            squares = squares + total * total

    own_sum = jnp.sum(squares, axis=1, keepdims=True)
    sq_own[...] = jnp.broadcast_to(
        jnp.sum(jnp.where(eye, own_sum, 0.0), axis=0, keepdims=True), sq_own.shape
    )

    def sq_copy(i):
        return remote(sq_own, sq_in.at[i], sq_s.at[i], sq_r.at[i], at(head=mates[i]))

    for i in range(3):
        sq_copy(i).start()
    sum_row = sq_own[0:1, :]
    for i in range(3):
        sq_copy(i).wait_recv()
        sum_row = sum_row + sq_in[i, 0:1, :]
    sum_col = jnp.sum(jnp.where(eye, sum_row, 0.0), axis=1, keepdims=True)
    inverse_rms = lax.rsqrt(sum_col / HDIM + epsilon)

    def row_copy(c, k):
        i = c * (SEQ - 1) + k - 1
        return remote(
            rows.at[c, z], rows.at[c, z], row_s.at[i], row_r.at[i], at(seq=lax.rem(z + k, SEQ))
        )

    for c in range(HALVES):
        here = slice(c * half, (c + 1) * half)
        rows[c, z] = (attended[here, :] * inverse_rms[here, :] * gain_ref[...]).astype(BF16)
        for k in range(1, SEQ):
            row_copy(c, k).start()

    TILE = 256
    depth = ow.shape[0]

    def project(c):
        for k in range(1, SEQ):
            row_copy(c, k).wait_recv()

        def one(n, carry):
            cols = pl.ds(pl.multiple_of(n * TILE, TILE), TILE)
            product = jnp.dot(
                rows[c].reshape(SEQ * half, depth), ow[:, cols], preferred_element_type=F32
            ).reshape(GROUP, half, TILE)
            part[:, :, cols] = product
            part_out[c, :, :, cols] = product.astype(BF16)
            return carry

        lax.fori_loop(0, width // TILE, one, 0)
        for i in range(3):
            part_copy(c, i).start()

    def part_copy(c, i):
        j = c * 3 + i
        return remote(
            part_out.at[c, mates[i]], part_in.at[c, i], part_s.at[j], part_r.at[j], at(head=mates[i])
        )

    def z_copy(c, k):
        i = c * (SEQ - 1) + k - 1
        block = feats.at[c, z, h]
        return remote(block, block, zg_s.at[i], zg_r.at[i], at(seq=lax.rem(z + k, SEQ)))

    def hand_copy(c):
        return remote(feats.at[c, z, h], hand_in.at[c], hand_s.at[c], hand_r.at[c], at(section=1 - s))

    def column(k):
        return lax.rem(z + SEQ - k, SEQ)

    def x_copy(c, k):
        i = c * SEQ + k
        block = feats.at[c, column(k), h]
        return remote(block, block, x_s.at[i], x_r.at[i], at(head=x_peer))

    def y_copy(c, k):
        i = c * SEQ + k
        block = feats.at[c, column(k), h]
        return remote(block, block, y_s.at[i], y_r.at[i], at(head=y_peer))

    def d_copy(c, k):
        i = c * SEQ + k
        source, target = (x_peer, y_peer) if k % 2 == 0 else (y_peer, x_peer)
        block = feats.at[c, column(k), source]
        return remote(block, block, d_s.at[i], d_r.at[i], at(head=target))

    def finish(c):
        here = slice(c * half, (c + 1) * half)
        total = res_ref[0, here, :].astype(F32) + own_part[c]
        for i in range(3):
            part_copy(c, i).wait_recv()
        for i in range(3):
            total = total + part_in[c, i].astype(F32)
        feats[c, z, h] = total.astype(BF16)
        for k in (2, 1, 3):
            z_copy(c, k).start()
        x_copy(c, 0).start()
        y_copy(c, 0).start()
        hand_copy(c).start()

    def relay(c, k):
        if k > 0:
            z_copy(c, k).wait_recv()
            x_copy(c, k).start()
            y_copy(c, k).start()

    def forward(c, k):
        (x_copy if k % 2 == 0 else y_copy)(c, k).wait_recv()
        d_copy(c, k).start()

    def encode(c, k):
        (y_copy if k % 2 == 0 else x_copy)(c, k).wait_recv()
        d_copy(c, k).wait_recv()
        which = column(k)
        depth_rows = pl.ds(pl.multiple_of(which * width, width), width)

        def one(n, carry):
            cols = pl.ds(pl.multiple_of(n * TILE, TILE), TILE)
            product = jnp.dot(
                feats[c, which].reshape(GROUP * half, width),
                enc[depth_rows, cols],
                preferred_element_type=F32,
            )
            if k == 0:
                acc[:, cols] = product + bias_ref[:, cols]
            elif k < SEQ - 1:
                acc[:, cols] += product
            else:
                latent = jnp.maximum(acc[:, cols] + product, 0.0)
                means = jnp.sum(latent.reshape(GROUP, half, TILE), axis=1) / POOL
                for j in range(GROUP):
                    pool[HALVES * j + c : HALVES * j + c + 1, cols] = means[j : j + 1, :]
            return carry

        lax.fori_loop(0, latents // TILE, one, 0)

    own_part = {}
    ow_copy.wait()
    for c in range(HALVES):
        project(c)
        own_part[c] = part[h]
        finish(c)
    enc_copy.wait()
    steps = [(c, k) for c in range(HALVES) for k in range(SEQ)]
    lead, lag = 2, 3
    for t in range(len(steps) + lag):
        if t < len(steps):
            relay(*steps[t])
        if 0 <= t - lead < len(steps):
            forward(*steps[t - lead])
        if 0 <= t - lag < len(steps):
            encode(*steps[t - lag])

    pool_copy = remote(pool, pool_in, pool_sem.at[0], pool_sem.at[1], at(section=1 - s))
    pool_copy.start()
    for c in range(HALVES):
        hand_copy(c).wait_recv()
        hand_ref[0, c * half : (c + 1) * half, :] = hand_in[c]
    pool_copy.wait_recv()
    mon_ref[0] = pool_in[...].astype(BF16)

    @pl.when(z < SEQ - 1)
    def _():
        doc_copy().wait_send()
        for c in range(HEAD_CHUNKS):
            state_copy(c).wait_send()

    pool_copy.wait_send()
    for i in range(3):
        sq_copy(i).wait_send()
    for c in range(HALVES):
        hand_copy(c).wait_send()
        for i in range(3):
            part_copy(c, i).wait_send()
        for k in range(1, SEQ):
            row_copy(c, k).wait_send()
            z_copy(c, k).wait_send()
        for k in range(SEQ):
            x_copy(c, k).wait_send()
            y_copy(c, k).wait_send()
            d_copy(c, k).wait_send()


def fused(
    query_vectors,
    key_vectors,
    value_vectors,
    prior_state,
    doc_ids,
    norm_gain,
    residual,
    out_weight,
    enc_weight,
    enc_bias,
):
    tokens, features = query_vectors.shape[1:]
    heads = features // HD
    width = residual.shape[2]
    depth, latents = enc_weight.shape[1:]
    half = tokens // HALVES
    per_chunk = heads // HEAD_CHUNKS
    vmem = pl.BlockSpec(memory_space=pltpu.VMEM)
    anywhere = pl.BlockSpec(memory_space=pl.ANY)
    dma = lambda n: pltpu.SemaphoreType.DMA((n,))
    buf = lambda shape, dtype: pltpu.VMEM(shape, dtype)
    return pl.pallas_call(
        fused_kernel,
        out_shape=(
            jax.ShapeDtypeStruct((1, tokens, width), BF16),
            jax.ShapeDtypeStruct((1, SEQ * HALVES, latents), BF16),
        ),
        in_specs=[vmem] * 7 + [anywhere] * 2 + [vmem],
        out_specs=(vmem, vmem),
        scratch_shapes=[
            buf((features, width), BF16),
            buf((depth, latents), BF16),
            buf((8, tokens), F32),
            buf((8, tokens), F32),
            buf((HEAD_CHUNKS, per_chunk, HD, HD), BF16),
            buf((HEAD_CHUNKS, per_chunk, HD, HD), BF16),
            buf((heads, HD, HD), F32),
            buf((tokens, features), F32),
            buf((8, tokens), F32),
            buf((3, 8, tokens), F32),
            buf((HALVES, SEQ, half, features), BF16),
            buf((GROUP, half, width), F32),
            buf((HALVES, GROUP, half, width), BF16),
            buf((HALVES, 3, half, width), BF16),
            buf((HALVES, SEQ, GROUP, half, width), BF16),
            buf((HALVES, half, width), BF16),
            buf((GROUP * half, latents), F32),
            buf((SEQ * HALVES, latents), F32),
            buf((SEQ * HALVES, latents), F32),
            pltpu.SemaphoreType.DMA,
            pltpu.SemaphoreType.DMA,
            dma(2),
            dma(HEAD_CHUNKS),
            dma(HEAD_CHUNKS),
            dma(3),
            dma(3),
            dma(HALVES * (SEQ - 1)),
            dma(HALVES * (SEQ - 1)),
            dma(HALVES * 3),
            dma(HALVES * 3),
            dma(HALVES * (SEQ - 1)),
            dma(HALVES * (SEQ - 1)),
            dma(HALVES * SEQ),
            dma(HALVES * SEQ),
            dma(HALVES * SEQ),
            dma(HALVES * SEQ),
            dma(HALVES * SEQ),
            dma(HALVES * SEQ),
            dma(HALVES),
            dma(HALVES),
            dma(2),
        ],
        compiler_params=pltpu.CompilerParams(
            collective_id=0, has_side_effects=True, vmem_limit_bytes=60 * 2**20
        ),
        name="section",
    )(
        query_vectors,
        key_vectors,
        value_vectors,
        prior_state,
        doc_ids,
        norm_gain,
        residual,
        out_weight,
        enc_weight,
        enc_bias,
    )


def solution(mesh):
    sizes = (mesh.shape["section"], mesh.shape["seq"], mesh.shape["head"])
    body = fused if sizes == (2, SEQ, GROUP) else local
    return jax.shard_map(
        body,
        mesh=mesh,
        in_specs=(
            P("section", "seq", "head"),
            P("section", "seq", "head"),
            P("section", "seq", "head"),
            P("section", "head", None, None),
            P("section", "seq"),
            P("section", "head"),
            P("section", "head", "seq"),
            P("section", "head", "seq"),
            P("section", None, ("seq", "head")),
            P("section", ("seq", "head")),
        ),
        out_specs=(P("section", "head", "seq"), P("section", None, ("seq", "head"))),
        check_vma=False,
    )
```

```python
import jax
import jax.numpy as jnp
from jax import lax
from jax.experimental import pallas as pl
from jax.experimental.pallas import tpu as pltpu
from jax.sharding import PartitionSpec as P

HD = 128
POOL = 64
HDIM = 8192


epsilon = 1e-06


def entering(part, axis, combine, identity):
    place = lax.axis_index(axis)
    gathered = jax.tree.map(lambda a: lax.all_gather(a, axis), part)
    state = jax.tree.map(lambda a, e: jnp.zeros_like(a) + jnp.asarray(e, a.dtype), part, identity)

    def one(hop, state):
        return combine(
            state, jax.tree.map(lambda a: lax.dynamic_index_in_dim(a, hop, 0, False), gathered)
        )

    return lax.fori_loop(0, place, one, state)


def passed_along(x, axis, by):
    devices = lax.axis_size(axis)
    return lax.ppermute(x, axis, [(i, (i + by) % devices) for i in range(devices)])


def merge_states(first_pair, second_pair):
    first_state, first_doc = first_pair
    second_state, second_doc = second_pair
    top_doc = jnp.maximum(first_doc, second_doc)
    merged = jnp.where(first_doc == top_doc, first_state, 0.0) + jnp.where(
        second_doc == top_doc, second_state, 0.0
    )
    return (merged, top_doc)


def local(
    query_vectors,
    key_vectors,
    value_vectors,
    prior_state,
    doc_ids,
    norm_gain,
    residual,
    out_weight,
    enc_weight,
    enc_bias,
):
    highest = lax.Precision.HIGHEST
    row_count = query_vectors.shape[1]
    local_heads = query_vectors.shape[2] // HD
    queries = query_vectors[0].reshape(row_count, local_heads, HD)
    keys_block = key_vectors[0].reshape(row_count, local_heads, HD)
    values_block = value_vectors[0].reshape(row_count, local_heads, HD)
    doc_index = doc_ids[0]
    doc_float = doc_index.astype(jnp.float32)
    last_doc = doc_float[-1]
    keys_last = jnp.where(
        (doc_index == doc_index[-1])[:, None, None], keys_block, jnp.zeros_like(keys_block)
    )
    summary = jnp.einsum(
        "thd,the->hde", keys_last, values_block, preferred_element_type=jnp.float32
    )
    identity_pair = (jnp.zeros_like(summary), jnp.full((1,), -1.0, jnp.float32))
    earlier_state, earlier_last = entering(
        (summary, last_doc[None]), "seq", merge_states, identity_pair
    )
    earlier_doc = earlier_last[0]
    incoming_state, incoming_doc = merge_states(
        (prior_state[0], jnp.zeros((), jnp.float32)), (earlier_state, earlier_doc)
    )
    inter = jnp.einsum(
        "thd,hde->the", queries.astype(jnp.float32), incoming_state, precision=highest
    )
    inter = inter * (doc_float == incoming_doc).astype(jnp.float32)[:, None, None]
    scores = jnp.einsum("thd,uhd->htu", queries, keys_block, preferred_element_type=jnp.float32)
    positions = jnp.arange(row_count)
    same_doc = (positions[None, :] <= positions[:, None]) & (
        doc_index[:, None] == doc_index[None, :]
    )
    scores = jnp.where(same_doc[None, :, :], scores, 0.0)
    intra = jnp.einsum("htu,uhe->the", scores, values_block.astype(jnp.float32), precision=highest)
    attended = (inter + intra).reshape(row_count, local_heads * HD)
    total_square = lax.psum(jnp.sum(attended * attended, axis=1), "head")
    inverse_rms = lax.rsqrt(total_square / HDIM + epsilon)
    normed = (attended * inverse_rms[:, None] * norm_gain[0]).astype(jnp.bfloat16)
    projection = out_weight[0]
    partial_sums = jnp.dot(
        lax.all_gather(normed, "seq", axis=0, tiled=True),
        projection,
        preferred_element_type=jnp.float32,
    )
    own_rows = residual[0]
    encoder = enc_weight[0]
    latent_width = encoder.shape[1]
    reduced = lax.psum_scatter(partial_sums, "head", scatter_dimension=0, tiled=True)
    layer_out = (own_rows.astype(jnp.float32) + reduced).astype(jnp.bfloat16)
    features = lax.all_gather(layer_out, "head", axis=0, tiled=True)
    pre_scores = jnp.dot(
        lax.all_gather(features, "seq", axis=1, tiled=True),
        encoder,
        preferred_element_type=jnp.float32,
    )
    latent = jax.nn.relu(pre_scores + enc_bias[0])
    pooled = jnp.mean(latent.reshape(-1, POOL, latent_width), axis=1).astype(jnp.bfloat16)
    handoff, monitor = passed_along((layer_out[None], pooled[None]), "section", 1)
    return (handoff, monitor)


MESH = pl.DeviceIdType.MESH
F32 = jnp.float32
BF16 = jnp.bfloat16
SEQ = 4
GROUP = 4
CHUNKS = 4
HEAD_GROUPS = 8


def fused_kernel(
    q_ref,
    k_ref,
    v_ref,
    prior_ref,
    doc_ref,
    gain_ref,
    res_ref,
    ow_hbm,
    enc_hbm,
    bias_ref,
    hand_ref,
    mon_ref,
    ow,
    enc,
    doc_own,
    doc_prev,
    state_in,
    state_out,
    summary,
    attended,
    sq_own,
    sq_in,
    rows,
    part,
    part_out,
    part_in,
    feats,
    hand_in,
    acc,
    pool,
    pool_in,
    ow_sem,
    enc_sem,
    doc_sem,
    st_s,
    st_r,
    sq_s,
    sq_r,
    row_s,
    row_r,
    part_s,
    part_r,
    zg_s,
    zg_r,
    x_s,
    x_r,
    y_s,
    y_r,
    d_s,
    d_r,
    hand_s,
    hand_r,
    pool_sem,
):
    s = lax.axis_index("section")
    z = lax.axis_index("seq")
    h = lax.axis_index("head")
    tokens = q_ref.shape[1]
    chunk_rows = tokens // CHUNKS
    heads = q_ref.shape[2] // HD
    per_chunk = heads // HEAD_GROUPS
    width = res_ref.shape[2]
    latents = bias_ref.shape[1]
    x_peer = h + 1 - 2 * lax.rem(h, 2)
    y_peer = lax.rem(h + 2, 4)
    d_peer = 3 - h
    mates = (x_peer, y_peer, d_peer)

    def at(seq=None, head=None, section=None):
        return (
            s if section is None else section,
            z if seq is None else seq,
            h if head is None else head,
        )

    def remote(src, dst, send, recv, device):
        return pltpu.make_async_remote_copy(
            src_ref=src, dst_ref=dst, send_sem=send, recv_sem=recv,
            device_id=device, device_id_type=MESH,
        )

    ow_copy = pltpu.make_async_copy(ow_hbm.at[0], ow, ow_sem)
    enc_copy = pltpu.make_async_copy(enc_hbm.at[0], enc, enc_sem)
    ow_copy.start()
    enc_copy.start()

    barrier = pltpu.get_barrier_semaphore()
    for k in range(1, SEQ):
        pl.semaphore_signal(barrier, inc=1, device_id=at(seq=lax.rem(z + k, SEQ)), device_id_type=MESH)
    for mate in mates:
        pl.semaphore_signal(barrier, inc=1, device_id=at(head=mate), device_id_type=MESH)
    pl.semaphore_signal(barrier, inc=1, device_id=at(section=1 - s), device_id_type=MESH)
    pl.semaphore_wait(barrier, SEQ - 1 + 3 + 1)

    row_iota = lax.broadcasted_iota(jnp.int32, (tokens, tokens), 0)
    col_iota = lax.broadcasted_iota(jnp.int32, (tokens, tokens), 1)
    eye = row_iota == col_iota
    doc_own[...] = jnp.broadcast_to(doc_ref[...].astype(F32), doc_own.shape)
    later = jnp.minimum(z + 1, SEQ - 1)

    def doc_copy():
        return remote(doc_own, doc_prev, doc_sem.at[0], doc_sem.at[1], at(seq=later))

    def state_copy(c):
        return remote(state_out.at[c], state_in.at[c], st_s.at[c], st_r.at[c], at(seq=later))

    @pl.when(z < SEQ - 1)
    def _():
        doc_copy().start()

    doc_row = doc_own[0:1, :]
    doc_col = jnp.sum(jnp.where(eye, doc_row, 0.0), axis=1, keepdims=True)
    last_doc = jnp.max(doc_row, axis=1, keepdims=True)
    keep_key = doc_col == last_doc
    same_doc = (doc_col == doc_row) & (col_iota <= row_iota)

    def columns(head):
        return slice(head * HD, (head + 1) * HD)

    def summarize(head):
        keys = k_ref[0, :, columns(head)]
        keys = jnp.where(keep_key, keys.astype(F32), 0.0).astype(BF16)
        summary[head] = lax.dot_general(
            keys, v_ref[0, :, columns(head)], (((0,), (0,)), ((), ())), preferred_element_type=F32
        )

    def within(head):
        cols = columns(head)
        values = v_ref[0, :, cols]
        scores = lax.dot_general(
            q_ref[0, :, cols], k_ref[0, :, cols], (((1,), (1,)), ((), ())), preferred_element_type=F32
        )
        scores = jnp.where(same_doc, scores, 0.0)
        high = scores.astype(BF16)
        low = (scores - high.astype(F32)).astype(BF16)
        attended[:, cols] = jnp.dot(high, values, preferred_element_type=F32) + jnp.dot(
            low, values, preferred_element_type=F32
        )

    def send_state(c):
        for i in range(per_chunk):
            head = c * per_chunk + i
            state_out[c, i] = (state_in[c, i].astype(F32) * carried + summary[head]).astype(BF16)
        state_copy(c).start()

    @pl.when(z == 0)
    def _():
        doc_prev[...] = jnp.zeros_like(doc_prev)

    @pl.when(z > 0)
    def _():
        doc_copy().wait_recv()

    entering_doc = jnp.max(doc_prev[0:1, :], axis=1, keepdims=True)
    carried = jnp.where(last_doc == entering_doc, 1.0, 0.0)
    from_before = jnp.where(doc_col == entering_doc, 1.0, 0.0)

    for c in range(HEAD_GROUPS):
        for i in range(per_chunk):
            summarize(c * per_chunk + i)

        @pl.when(z == 0)
        def _():
            state_in[c] = prior_ref[0, c * per_chunk : (c + 1) * per_chunk].astype(BF16)
            send_state(c)

    squares = jnp.zeros((tokens, HD), F32)
    for c in range(HEAD_GROUPS):
        @pl.when(z > 0)
        def _():
            state_copy(c).wait_recv()

        @pl.when((z > 0) & (z < SEQ - 1))
        def _():
            send_state(c)

        for i in range(per_chunk):
            head = c * per_chunk + i
            cols = columns(head)
            within(head)
            inter = jnp.dot(q_ref[0, :, cols], state_in[c, i], preferred_element_type=F32)
            total = attended[:, cols] + inter * from_before
            attended[:, cols] = total
            squares = squares + total * total

    own_sum = jnp.sum(squares, axis=1, keepdims=True)
    sq_own[...] = jnp.broadcast_to(
        jnp.sum(jnp.where(eye, own_sum, 0.0), axis=0, keepdims=True), sq_own.shape
    )

    def sq_copy(i):
        return remote(sq_own, sq_in.at[i], sq_s.at[i], sq_r.at[i], at(head=mates[i]))

    for i in range(3):
        sq_copy(i).start()
    sum_row = sq_own[0:1, :]
    for i in range(3):
        sq_copy(i).wait_recv()
        sum_row = sum_row + sq_in[i, 0:1, :]
    sum_col = jnp.sum(jnp.where(eye, sum_row, 0.0), axis=1, keepdims=True)
    inverse_rms = lax.rsqrt(sum_col / HDIM + epsilon)

    def row_copy(c, k):
        i = c * (SEQ - 1) + k - 1
        return remote(
            rows.at[c, z], rows.at[c, z], row_s.at[i], row_r.at[i], at(seq=lax.rem(z + k, SEQ))
        )

    def push_rows(c):
        for k in (2, 1, 3):
            row_copy(c, k).start()

    for c in range(CHUNKS):
        here = slice(c * chunk_rows, (c + 1) * chunk_rows)
        rows[c, z] = (attended[here, :] * inverse_rms[here, :] * gain_ref[...]).astype(BF16)
        if c < 2:
            push_rows(c)

    TILE = 256
    depth = ow.shape[0]

    def project(c):
        for k in range(1, SEQ):
            row_copy(c, k).wait_recv()

        def one(n, carry):
            cols = pl.ds(pl.multiple_of(n * TILE, TILE), TILE)
            product = jnp.dot(
                rows[c].reshape(SEQ * chunk_rows, depth), ow[:, cols], preferred_element_type=F32
            ).reshape(GROUP, chunk_rows, TILE)
            part[:, :, cols] = product
            part_out[c, :, :, cols] = product.astype(BF16)
            return carry

        lax.fori_loop(0, width // TILE, one, 0)
        for i in range(3):
            part_copy(c, i).start()

    def part_copy(c, i):
        j = c * 3 + i
        return remote(
            part_out.at[c, mates[i]], part_in.at[c, i], part_s.at[j], part_r.at[j], at(head=mates[i])
        )

    def z_copy(c, k):
        i = c * (SEQ - 1) + k - 1
        block = feats.at[c, z, h]
        return remote(block, block, zg_s.at[i], zg_r.at[i], at(seq=lax.rem(z + k, SEQ)))

    def hand_copy(c):
        return remote(feats.at[c, z, h], hand_in.at[c], hand_s.at[c], hand_r.at[c], at(section=1 - s))

    def column(k):
        return lax.rem(z + SEQ - k, SEQ)

    def x_copy(c, k):
        i = c * SEQ + k
        block = feats.at[c, column(k), h]
        return remote(block, block, x_s.at[i], x_r.at[i], at(head=x_peer))

    def y_copy(c, k):
        i = c * SEQ + k
        block = feats.at[c, column(k), h]
        return remote(block, block, y_s.at[i], y_r.at[i], at(head=y_peer))

    def d_copy(c, k):
        i = c * SEQ + k
        source, target = (x_peer, y_peer) if k % 2 == 0 else (y_peer, x_peer)
        block = feats.at[c, column(k), source]
        return remote(block, block, d_s.at[i], d_r.at[i], at(head=target))

    def finish(c):
        here = slice(c * chunk_rows, (c + 1) * chunk_rows)
        total = res_ref[0, here, :].astype(F32) + own_part[c]
        for i in range(3):
            part_copy(c, i).wait_recv()
        for i in range(3):
            total = total + part_in[c, i].astype(F32)
        feats[c, z, h] = total.astype(BF16)
        for k in (2, 1, 3):
            z_copy(c, k).start()
        x_copy(c, 0).start()
        y_copy(c, 0).start()
        hand_copy(c).start()
        if c + 2 < CHUNKS:
            push_rows(c + 2)

    def relay(c):
        for k in range(1, SEQ):
            z_copy(c, k).wait_recv()
            x_copy(c, k).start()
            y_copy(c, k).start()

    def forward(c, k):
        (x_copy if k % 2 == 0 else y_copy)(c, k).wait_recv()
        d_copy(c, k).start()

    def encode(c, k):
        (y_copy if k % 2 == 0 else x_copy)(c, k).wait_recv()
        d_copy(c, k).wait_recv()
        which = column(k)
        depth_rows = pl.ds(pl.multiple_of(which * width, width), width)

        def one(n, carry):
            cols = pl.ds(pl.multiple_of(n * TILE, TILE), TILE)
            product = jnp.dot(
                feats[c, which].reshape(GROUP * chunk_rows, width),
                enc[depth_rows, cols],
                preferred_element_type=F32,
            )
            if k == 0:
                acc[:, cols] = product + bias_ref[:, cols]
            elif k < SEQ - 1:
                acc[:, cols] += product
            else:
                latent = jnp.maximum(acc[:, cols] + product, 0.0)
                sums = jnp.sum(latent.reshape(GROUP, chunk_rows, TILE), axis=1)
                for j in range(GROUP):
                    r = (j * tokens + c * chunk_rows) // POOL
                    row = sums[j : j + 1, :]
                    if c * chunk_rows % POOL:
                        row = row + pool[r : r + 1, cols]
                    if (c + 1) * chunk_rows % POOL == 0:
                        row = row / POOL
                    pool[r : r + 1, cols] = row
            return carry

        lax.fori_loop(0, latents // TILE, one, 0)

    own_part = {}

    def produce(c):
        project(c)
        own_part[c] = part[h]
        finish(c)

    def pass_on(c):
        for k in range(SEQ):
            forward(c, k)

    ow_copy.wait()
    produce(0)
    produce(1)
    relay(0)
    pass_on(0)
    produce(2)
    relay(1)
    pass_on(1)
    produce(3)
    relay(2)
    enc_copy.wait()
    for c in (0, 1):
        if c == 1:
            relay(3)
        for k in range(SEQ):
            encode(c, k)
            forward(c + 2, k)
    for c in (2, 3):
        for k in range(SEQ):
            encode(c, k)

    pool_copy = remote(pool, pool_in, pool_sem.at[0], pool_sem.at[1], at(section=1 - s))
    pool_copy.start()
    for c in range(CHUNKS):
        hand_copy(c).wait_recv()
        hand_ref[0, c * chunk_rows : (c + 1) * chunk_rows, :] = hand_in[c]
    pool_copy.wait_recv()
    mon_ref[0] = pool_in[...].astype(BF16)

    @pl.when(z < SEQ - 1)
    def _():
        doc_copy().wait_send()
        for c in range(HEAD_GROUPS):
            state_copy(c).wait_send()

    pool_copy.wait_send()
    for i in range(3):
        sq_copy(i).wait_send()
    for c in range(CHUNKS):
        hand_copy(c).wait_send()
        for i in range(3):
            part_copy(c, i).wait_send()
        for k in range(1, SEQ):
            row_copy(c, k).wait_send()
            z_copy(c, k).wait_send()
        for k in range(SEQ):
            x_copy(c, k).wait_send()
            y_copy(c, k).wait_send()
            d_copy(c, k).wait_send()


def fused(
    query_vectors,
    key_vectors,
    value_vectors,
    prior_state,
    doc_ids,
    norm_gain,
    residual,
    out_weight,
    enc_weight,
    enc_bias,
):
    tokens, features = query_vectors.shape[1:]
    heads = features // HD
    width = residual.shape[2]
    depth, latents = enc_weight.shape[1:]
    chunk_rows = tokens // CHUNKS
    per_chunk = heads // HEAD_GROUPS
    vmem = pl.BlockSpec(memory_space=pltpu.VMEM)
    anywhere = pl.BlockSpec(memory_space=pl.ANY)
    dma = lambda n: pltpu.SemaphoreType.DMA((n,))
    buf = lambda shape, dtype: pltpu.VMEM(shape, dtype)
    return pl.pallas_call(
        fused_kernel,
        out_shape=(
            jax.ShapeDtypeStruct((1, tokens, width), BF16),
            jax.ShapeDtypeStruct((1, SEQ * tokens // POOL, latents), BF16),
        ),
        in_specs=[vmem] * 7 + [anywhere] * 2 + [vmem],
        out_specs=(vmem, vmem),
        scratch_shapes=[
            buf((features, width), BF16),
            buf((depth, latents), BF16),
            buf((8, tokens), F32),
            buf((8, tokens), F32),
            buf((HEAD_GROUPS, per_chunk, HD, HD), BF16),
            buf((HEAD_GROUPS, per_chunk, HD, HD), BF16),
            buf((heads, HD, HD), F32),
            buf((tokens, features), F32),
            buf((8, tokens), F32),
            buf((3, 8, tokens), F32),
            buf((CHUNKS, SEQ, chunk_rows, features), BF16),
            buf((GROUP, chunk_rows, width), F32),
            buf((CHUNKS, GROUP, chunk_rows, width), BF16),
            buf((CHUNKS, 3, chunk_rows, width), BF16),
            buf((CHUNKS, SEQ, GROUP, chunk_rows, width), BF16),
            buf((CHUNKS, chunk_rows, width), BF16),
            buf((GROUP * chunk_rows, latents), F32),
            buf((SEQ * tokens // POOL, latents), F32),
            buf((SEQ * tokens // POOL, latents), F32),
            pltpu.SemaphoreType.DMA,
            pltpu.SemaphoreType.DMA,
            dma(2),
            dma(HEAD_GROUPS),
            dma(HEAD_GROUPS),
            dma(3),
            dma(3),
            dma(CHUNKS * (SEQ - 1)),
            dma(CHUNKS * (SEQ - 1)),
            dma(CHUNKS * 3),
            dma(CHUNKS * 3),
            dma(CHUNKS * (SEQ - 1)),
            dma(CHUNKS * (SEQ - 1)),
            dma(CHUNKS * SEQ),
            dma(CHUNKS * SEQ),
            dma(CHUNKS * SEQ),
            dma(CHUNKS * SEQ),
            dma(CHUNKS * SEQ),
            dma(CHUNKS * SEQ),
            dma(CHUNKS),
            dma(CHUNKS),
            dma(2),
        ],
        compiler_params=pltpu.CompilerParams(
            collective_id=0, has_side_effects=True, vmem_limit_bytes=60 * 2**20
        ),
        name="section",
    )(
        query_vectors,
        key_vectors,
        value_vectors,
        prior_state,
        doc_ids,
        norm_gain,
        residual,
        out_weight,
        enc_weight,
        enc_bias,
    )


def solution(mesh):
    sizes = (mesh.shape["section"], mesh.shape["seq"], mesh.shape["head"])
    body = fused if sizes == (2, SEQ, GROUP) else local
    return jax.shard_map(
        body,
        mesh=mesh,
        in_specs=(
            P("section", "seq", "head"),
            P("section", "seq", "head"),
            P("section", "seq", "head"),
            P("section", "head", None, None),
            P("section", "seq"),
            P("section", "head"),
            P("section", "head", "seq"),
            P("section", "head", "seq"),
            P("section", None, ("seq", "head")),
            P("section", ("seq", "head")),
        ),
        out_specs=(P("section", "head", "seq"), P("section", None, ("seq", "head"))),
        check_vma=False,
    )
```

```python
import jax
import jax.numpy as jnp
from jax import lax
from jax.experimental import pallas as pl
from jax.experimental.pallas import tpu as pltpu
from jax.sharding import PartitionSpec as P

HD = 128
POOL = 64
HDIM = 8192


epsilon = 1e-06


def entering(part, axis, combine, identity):
    place = lax.axis_index(axis)
    gathered = jax.tree.map(lambda a: lax.all_gather(a, axis), part)
    state = jax.tree.map(lambda a, e: jnp.zeros_like(a) + jnp.asarray(e, a.dtype), part, identity)

    def one(hop, state):
        return combine(
            state, jax.tree.map(lambda a: lax.dynamic_index_in_dim(a, hop, 0, False), gathered)
        )

    return lax.fori_loop(0, place, one, state)


def passed_along(x, axis, by):
    devices = lax.axis_size(axis)
    return lax.ppermute(x, axis, [(i, (i + by) % devices) for i in range(devices)])


def merge_states(first_pair, second_pair):
    first_state, first_doc = first_pair
    second_state, second_doc = second_pair
    top_doc = jnp.maximum(first_doc, second_doc)
    merged = jnp.where(first_doc == top_doc, first_state, 0.0) + jnp.where(
        second_doc == top_doc, second_state, 0.0
    )
    return (merged, top_doc)


def local(
    query_vectors,
    key_vectors,
    value_vectors,
    prior_state,
    doc_ids,
    norm_gain,
    residual,
    out_weight,
    enc_weight,
    enc_bias,
):
    highest = lax.Precision.HIGHEST
    row_count = query_vectors.shape[1]
    local_heads = query_vectors.shape[2] // HD
    queries = query_vectors[0].reshape(row_count, local_heads, HD)
    keys_block = key_vectors[0].reshape(row_count, local_heads, HD)
    values_block = value_vectors[0].reshape(row_count, local_heads, HD)
    doc_index = doc_ids[0]
    doc_float = doc_index.astype(jnp.float32)
    last_doc = doc_float[-1]
    keys_last = jnp.where(
        (doc_index == doc_index[-1])[:, None, None], keys_block, jnp.zeros_like(keys_block)
    )
    summary = jnp.einsum(
        "thd,the->hde", keys_last, values_block, preferred_element_type=jnp.float32
    )
    identity_pair = (jnp.zeros_like(summary), jnp.full((1,), -1.0, jnp.float32))
    earlier_state, earlier_last = entering(
        (summary, last_doc[None]), "seq", merge_states, identity_pair
    )
    earlier_doc = earlier_last[0]
    incoming_state, incoming_doc = merge_states(
        (prior_state[0], jnp.zeros((), jnp.float32)), (earlier_state, earlier_doc)
    )
    inter = jnp.einsum(
        "thd,hde->the", queries.astype(jnp.float32), incoming_state, precision=highest
    )
    inter = inter * (doc_float == incoming_doc).astype(jnp.float32)[:, None, None]
    scores = jnp.einsum("thd,uhd->htu", queries, keys_block, preferred_element_type=jnp.float32)
    positions = jnp.arange(row_count)
    same_doc = (positions[None, :] <= positions[:, None]) & (
        doc_index[:, None] == doc_index[None, :]
    )
    scores = jnp.where(same_doc[None, :, :], scores, 0.0)
    intra = jnp.einsum("htu,uhe->the", scores, values_block.astype(jnp.float32), precision=highest)
    attended = (inter + intra).reshape(row_count, local_heads * HD)
    total_square = lax.psum(jnp.sum(attended * attended, axis=1), "head")
    inverse_rms = lax.rsqrt(total_square / HDIM + epsilon)
    normed = (attended * inverse_rms[:, None] * norm_gain[0]).astype(jnp.bfloat16)
    projection = out_weight[0]
    partial_sums = jnp.dot(
        lax.all_gather(normed, "seq", axis=0, tiled=True),
        projection,
        preferred_element_type=jnp.float32,
    )
    own_rows = residual[0]
    encoder = enc_weight[0]
    latent_width = encoder.shape[1]
    reduced = lax.psum_scatter(partial_sums, "head", scatter_dimension=0, tiled=True)
    layer_out = (own_rows.astype(jnp.float32) + reduced).astype(jnp.bfloat16)
    features = lax.all_gather(layer_out, "head", axis=0, tiled=True)
    pre_scores = jnp.dot(
        lax.all_gather(features, "seq", axis=1, tiled=True),
        encoder,
        preferred_element_type=jnp.float32,
    )
    latent = jax.nn.relu(pre_scores + enc_bias[0])
    pooled = jnp.mean(latent.reshape(-1, POOL, latent_width), axis=1).astype(jnp.bfloat16)
    handoff, monitor = passed_along((layer_out[None], pooled[None]), "section", 1)
    return (handoff, monitor)


MESH = pl.DeviceIdType.MESH
F32 = jnp.float32
BF16 = jnp.bfloat16
SEQ = 4
GROUP = 4
CHUNKS = 4
HEAD_GROUPS = 8


def fused_kernel(
    q_ref,
    k_ref,
    v_ref,
    prior_ref,
    doc_ref,
    gain_ref,
    res_ref,
    ow_hbm,
    enc_hbm,
    bias_ref,
    hand_ref,
    mon_ref,
    ow,
    enc,
    doc_own,
    doc_prev,
    state_in,
    state_out,
    summary,
    attended,
    sq_own,
    sq_in,
    rows,
    part,
    part_out,
    part_in,
    feats,
    hand_in,
    acc,
    pool,
    pool_in,
    ow_sem,
    enc_sem,
    doc_sem,
    st_s,
    st_r,
    sq_s,
    sq_r,
    row_s,
    row_r,
    part_s,
    part_r,
    zg_s,
    zg_r,
    x_s,
    x_r,
    y_s,
    y_r,
    d_s,
    d_r,
    hand_s,
    hand_r,
    pool_sem,
):
    s = lax.axis_index("section")
    z = lax.axis_index("seq")
    h = lax.axis_index("head")
    tokens = q_ref.shape[1]
    chunk_rows = tokens // CHUNKS
    heads = q_ref.shape[2] // HD
    per_chunk = heads // HEAD_GROUPS
    width = res_ref.shape[2]
    latents = bias_ref.shape[1]
    x_peer = h + 1 - 2 * lax.rem(h, 2)
    y_peer = lax.rem(h + 2, 4)
    d_peer = 3 - h
    mates = (x_peer, y_peer, d_peer)

    def at(seq=None, head=None, section=None):
        return (
            s if section is None else section,
            z if seq is None else seq,
            h if head is None else head,
        )

    def remote(src, dst, send, recv, device):
        return pltpu.make_async_remote_copy(
            src_ref=src, dst_ref=dst, send_sem=send, recv_sem=recv,
            device_id=device, device_id_type=MESH,
        )

    ow_copy = pltpu.make_async_copy(ow_hbm.at[0], ow, ow_sem)
    enc_copy = pltpu.make_async_copy(enc_hbm.at[0], enc, enc_sem)
    ow_copy.start()
    enc_copy.start()

    barrier = pltpu.get_barrier_semaphore()
    for k in range(1, SEQ):
        pl.semaphore_signal(barrier, inc=1, device_id=at(seq=lax.rem(z + k, SEQ)), device_id_type=MESH)
    for mate in mates:
        pl.semaphore_signal(barrier, inc=1, device_id=at(head=mate), device_id_type=MESH)
    pl.semaphore_signal(barrier, inc=1, device_id=at(section=1 - s), device_id_type=MESH)
    pl.semaphore_wait(barrier, SEQ - 1 + 3 + 1)

    row_iota = lax.broadcasted_iota(jnp.int32, (tokens, tokens), 0)
    col_iota = lax.broadcasted_iota(jnp.int32, (tokens, tokens), 1)
    eye = row_iota == col_iota
    doc_own[...] = jnp.broadcast_to(doc_ref[...].astype(F32), doc_own.shape)
    later = jnp.minimum(z + 1, SEQ - 1)

    def doc_copy():
        return remote(doc_own, doc_prev, doc_sem.at[0], doc_sem.at[1], at(seq=later))

    def state_copy(c):
        return remote(state_out.at[c], state_in.at[c], st_s.at[c], st_r.at[c], at(seq=later))

    @pl.when(z < SEQ - 1)
    def _():
        doc_copy().start()

    doc_row = doc_own[0:1, :]
    doc_col = jnp.sum(jnp.where(eye, doc_row, 0.0), axis=1, keepdims=True)
    last_doc = jnp.max(doc_row, axis=1, keepdims=True)
    keep_key = doc_col == last_doc
    same_doc = (doc_col == doc_row) & (col_iota <= row_iota)

    def columns(head):
        return slice(head * HD, (head + 1) * HD)

    def summarize(head):
        keys = k_ref[0, :, columns(head)]
        keys = jnp.where(keep_key, keys.astype(F32), 0.0).astype(BF16)
        summary[head] = lax.dot_general(
            keys, v_ref[0, :, columns(head)], (((0,), (0,)), ((), ())), preferred_element_type=F32
        )

    def within(head):
        cols = columns(head)
        values = v_ref[0, :, cols]
        scores = lax.dot_general(
            q_ref[0, :, cols], k_ref[0, :, cols], (((1,), (1,)), ((), ())), preferred_element_type=F32
        )
        scores = jnp.where(same_doc, scores, 0.0)
        high = scores.astype(BF16)
        low = (scores - high.astype(F32)).astype(BF16)
        attended[:, cols] = jnp.dot(high, values, preferred_element_type=F32) + jnp.dot(
            low, values, preferred_element_type=F32
        )

    def send_state(c):
        for i in range(per_chunk):
            head = c * per_chunk + i
            state_out[c, i] = (state_in[c, i].astype(F32) * carried + summary[head]).astype(BF16)
        state_copy(c).start()

    @pl.when(z == 0)
    def _():
        doc_prev[...] = jnp.zeros_like(doc_prev)

    @pl.when(z > 0)
    def _():
        doc_copy().wait_recv()

    entering_doc = jnp.max(doc_prev[0:1, :], axis=1, keepdims=True)
    carried = jnp.where(last_doc == entering_doc, 1.0, 0.0)
    from_before = jnp.where(doc_col == entering_doc, 1.0, 0.0)

    for c in range(HEAD_GROUPS):
        for i in range(per_chunk):
            summarize(c * per_chunk + i)

        @pl.when(z == 0)
        def _():
            state_in[c] = prior_ref[0, c * per_chunk : (c + 1) * per_chunk].astype(BF16)
            send_state(c)

    squares = jnp.zeros((tokens, HD), F32)
    for c in range(HEAD_GROUPS):
        @pl.when(z > 0)
        def _():
            state_copy(c).wait_recv()

        @pl.when((z > 0) & (z < SEQ - 1))
        def _():
            send_state(c)

        for i in range(per_chunk):
            head = c * per_chunk + i
            cols = columns(head)
            within(head)
            inter = jnp.dot(q_ref[0, :, cols], state_in[c, i], preferred_element_type=F32)
            total = attended[:, cols] + inter * from_before
            attended[:, cols] = total
            squares = squares + total * total

    own_sum = jnp.sum(squares, axis=1, keepdims=True)
    sq_own[...] = jnp.broadcast_to(
        jnp.sum(jnp.where(eye, own_sum, 0.0), axis=0, keepdims=True), sq_own.shape
    )

    def sq_copy(i):
        return remote(sq_own, sq_in.at[i], sq_s.at[i], sq_r.at[i], at(head=mates[i]))

    for i in range(3):
        sq_copy(i).start()
    sum_row = sq_own[0:1, :]
    for i in range(3):
        sq_copy(i).wait_recv()
        sum_row = sum_row + sq_in[i, 0:1, :]
    sum_col = jnp.sum(jnp.where(eye, sum_row, 0.0), axis=1, keepdims=True)
    inverse_rms = lax.rsqrt(sum_col / HDIM + epsilon)

    def row_copy(c, k):
        i = c * (SEQ - 1) + k - 1
        return remote(
            rows.at[c, z], rows.at[c, z], row_s.at[i], row_r.at[i], at(seq=lax.rem(z + k, SEQ))
        )

    inner = (z > 0) & (z < SEQ - 1)
    direct = {1: z != SEQ - 1, 2: z >= 0, 3: z != 0}
    relay_target = lax.rem(jnp.maximum(z - 1, 0), 2) * (SEQ - 1)
    relay_sem = lax.rem(2 * z + SEQ - 2, SEQ)
    relay_block = lax.rem(z + 2, SEQ)

    def start_along(copy, c):
        copy(c, 2).start()
        for k in (1, 3):

            @pl.when(direct[k])
            def _():
                copy(c, k).start()

    def wait_along(copy, relayed, c):
        copy(c, 2).wait_recv()

        @pl.when(inner)
        def _():
            relayed(c).start()

        for k in (1, 3):
            copy(c, k).wait_recv()

    def sent_along(copy, relayed, c):
        copy(c, 2).wait_send()
        for k in (1, 3):

            @pl.when(direct[k])
            def _():
                copy(c, k).wait_send()

        @pl.when(inner)
        def _():
            relayed(c).wait_send()

    def row_relay(c):
        block = rows.at[c, relay_block]
        return remote(
            block, block, row_s.at[CHUNKS * (SEQ - 1) + c],
            row_r.at[c * (SEQ - 1) + relay_sem], at(seq=relay_target),
        )

    def z_relay(c):
        block = feats.at[c, relay_block, h]
        return remote(
            block, block, zg_s.at[CHUNKS * (SEQ - 1) + c],
            zg_r.at[c * (SEQ - 1) + relay_sem], at(seq=relay_target),
        )

    def push_rows(c):
        start_along(row_copy, c)

    for c in range(CHUNKS):
        here = slice(c * chunk_rows, (c + 1) * chunk_rows)
        rows[c, z] = (attended[here, :] * inverse_rms[here, :] * gain_ref[...]).astype(BF16)
        if c < 2:
            push_rows(c)

    TILE = 256
    depth = ow.shape[0]

    def project(c):
        wait_along(row_copy, row_relay, c)

        def one(n, carry):
            cols = pl.ds(pl.multiple_of(n * TILE, TILE), TILE)
            product = jnp.dot(
                rows[c].reshape(SEQ * chunk_rows, depth), ow[:, cols], preferred_element_type=F32
            ).reshape(GROUP, chunk_rows, TILE)
            part[:, :, cols] = product
            part_out[c, :, :, cols] = product.astype(BF16)
            return carry

        lax.fori_loop(0, width // TILE, one, 0)
        for i in range(3):
            part_copy(c, i).start()

    def part_copy(c, i):
        j = c * 3 + i
        return remote(
            part_out.at[c, mates[i]], part_in.at[c, i], part_s.at[j], part_r.at[j], at(head=mates[i])
        )

    def z_copy(c, k):
        i = c * (SEQ - 1) + k - 1
        block = feats.at[c, z, h]
        return remote(block, block, zg_s.at[i], zg_r.at[i], at(seq=lax.rem(z + k, SEQ)))

    def hand_copy(c):
        return remote(feats.at[c, z, h], hand_in.at[c], hand_s.at[c], hand_r.at[c], at(section=1 - s))

    def column(k):
        return lax.rem(z + SEQ - k, SEQ)

    def x_copy(c, k):
        i = c * SEQ + k
        block = feats.at[c, column(k), h]
        return remote(block, block, x_s.at[i], x_r.at[i], at(head=x_peer))

    def y_copy(c, k):
        i = c * SEQ + k
        block = feats.at[c, column(k), h]
        return remote(block, block, y_s.at[i], y_r.at[i], at(head=y_peer))

    def d_copy(c, k):
        i = c * SEQ + k
        source, target = (x_peer, y_peer) if k % 2 == 0 else (y_peer, x_peer)
        block = feats.at[c, column(k), source]
        return remote(block, block, d_s.at[i], d_r.at[i], at(head=target))

    def finish(c):
        here = slice(c * chunk_rows, (c + 1) * chunk_rows)
        total = res_ref[0, here, :].astype(F32) + own_part[c]
        for i in range(3):
            part_copy(c, i).wait_recv()
        for i in range(3):
            total = total + part_in[c, i].astype(F32)
        feats[c, z, h] = total.astype(BF16)
        start_along(z_copy, c)
        x_copy(c, 0).start()
        y_copy(c, 0).start()
        hand_copy(c).start()
        if c + 2 < CHUNKS:
            push_rows(c + 2)

    def relay(c):
        wait_along(z_copy, z_relay, c)
        for k in range(1, SEQ):
            x_copy(c, k).start()
            y_copy(c, k).start()

    def forward(c, k):
        (x_copy if k % 2 == 0 else y_copy)(c, k).wait_recv()
        d_copy(c, k).start()

    def encode(c, k):
        (y_copy if k % 2 == 0 else x_copy)(c, k).wait_recv()
        d_copy(c, k).wait_recv()
        which = column(k)
        depth_rows = pl.ds(pl.multiple_of(which * width, width), width)

        def one(n, carry):
            cols = pl.ds(pl.multiple_of(n * TILE, TILE), TILE)
            product = jnp.dot(
                feats[c, which].reshape(GROUP * chunk_rows, width),
                enc[depth_rows, cols],
                preferred_element_type=F32,
            )
            if k == 0:
                acc[:, cols] = product + bias_ref[:, cols]
            elif k < SEQ - 1:
                acc[:, cols] += product
            else:
                latent = jnp.maximum(acc[:, cols] + product, 0.0)
                sums = jnp.sum(latent.reshape(GROUP, chunk_rows, TILE), axis=1)
                for j in range(GROUP):
                    r = (j * tokens + c * chunk_rows) // POOL
                    row = sums[j : j + 1, :]
                    if c * chunk_rows % POOL:
                        row = row + pool[r : r + 1, cols]
                    if (c + 1) * chunk_rows % POOL == 0:
                        row = row / POOL
                    pool[r : r + 1, cols] = row
            return carry

        lax.fori_loop(0, latents // TILE, one, 0)

    own_part = {}

    def produce(c):
        project(c)
        own_part[c] = part[h]
        finish(c)

    def pass_on(c):
        for k in range(SEQ):
            forward(c, k)

    ow_copy.wait()
    produce(0)
    produce(1)
    relay(0)
    pass_on(0)
    produce(2)
    relay(1)
    pass_on(1)
    enc_copy.wait()
    encode(0, 0)
    encode(0, 1)
    produce(3)
    relay(2)
    forward(2, 0)
    forward(2, 1)
    encode(0, 2)
    forward(2, 2)
    encode(0, 3)
    forward(2, 3)
    relay(3)
    for k in range(SEQ):
        forward(3, k)
        encode(1, k)
    for c in (2, 3):
        for k in range(SEQ):
            encode(c, k)

    pool_copy = remote(pool, pool_in, pool_sem.at[0], pool_sem.at[1], at(section=1 - s))
    pool_copy.start()
    for c in range(CHUNKS):
        hand_copy(c).wait_recv()
        hand_ref[0, c * chunk_rows : (c + 1) * chunk_rows, :] = hand_in[c]
    pool_copy.wait_recv()
    mon_ref[0] = pool_in[...].astype(BF16)

    @pl.when(z < SEQ - 1)
    def _():
        doc_copy().wait_send()
        for c in range(HEAD_GROUPS):
            state_copy(c).wait_send()

    pool_copy.wait_send()
    for i in range(3):
        sq_copy(i).wait_send()
    for c in range(CHUNKS):
        hand_copy(c).wait_send()
        for i in range(3):
            part_copy(c, i).wait_send()
        sent_along(row_copy, row_relay, c)
        sent_along(z_copy, z_relay, c)
        for k in range(SEQ):
            x_copy(c, k).wait_send()
            y_copy(c, k).wait_send()
            d_copy(c, k).wait_send()


def fused(
    query_vectors,
    key_vectors,
    value_vectors,
    prior_state,
    doc_ids,
    norm_gain,
    residual,
    out_weight,
    enc_weight,
    enc_bias,
):
    tokens, features = query_vectors.shape[1:]
    heads = features // HD
    width = residual.shape[2]
    depth, latents = enc_weight.shape[1:]
    chunk_rows = tokens // CHUNKS
    per_chunk = heads // HEAD_GROUPS
    vmem = pl.BlockSpec(memory_space=pltpu.VMEM)
    anywhere = pl.BlockSpec(memory_space=pl.ANY)
    dma = lambda n: pltpu.SemaphoreType.DMA((n,))
    buf = lambda shape, dtype: pltpu.VMEM(shape, dtype)
    return pl.pallas_call(
        fused_kernel,
        out_shape=(
            jax.ShapeDtypeStruct((1, tokens, width), BF16),
            jax.ShapeDtypeStruct((1, SEQ * tokens // POOL, latents), BF16),
        ),
        in_specs=[vmem] * 7 + [anywhere] * 2 + [vmem],
        out_specs=(vmem, vmem),
        scratch_shapes=[
            buf((features, width), BF16),
            buf((depth, latents), BF16),
            buf((8, tokens), F32),
            buf((8, tokens), F32),
            buf((HEAD_GROUPS, per_chunk, HD, HD), BF16),
            buf((HEAD_GROUPS, per_chunk, HD, HD), BF16),
            buf((heads, HD, HD), F32),
            buf((tokens, features), F32),
            buf((8, tokens), F32),
            buf((3, 8, tokens), F32),
            buf((CHUNKS, SEQ, chunk_rows, features), BF16),
            buf((GROUP, chunk_rows, width), F32),
            buf((CHUNKS, GROUP, chunk_rows, width), BF16),
            buf((CHUNKS, 3, chunk_rows, width), BF16),
            buf((CHUNKS, SEQ, GROUP, chunk_rows, width), BF16),
            buf((CHUNKS, chunk_rows, width), BF16),
            buf((GROUP * chunk_rows, latents), F32),
            buf((SEQ * tokens // POOL, latents), F32),
            buf((SEQ * tokens // POOL, latents), F32),
            pltpu.SemaphoreType.DMA,
            pltpu.SemaphoreType.DMA,
            dma(2),
            dma(HEAD_GROUPS),
            dma(HEAD_GROUPS),
            dma(3),
            dma(3),
            dma(CHUNKS * SEQ),
            dma(CHUNKS * (SEQ - 1)),
            dma(CHUNKS * 3),
            dma(CHUNKS * 3),
            dma(CHUNKS * SEQ),
            dma(CHUNKS * (SEQ - 1)),
            dma(CHUNKS * SEQ),
            dma(CHUNKS * SEQ),
            dma(CHUNKS * SEQ),
            dma(CHUNKS * SEQ),
            dma(CHUNKS * SEQ),
            dma(CHUNKS * SEQ),
            dma(CHUNKS),
            dma(CHUNKS),
            dma(2),
        ],
        compiler_params=pltpu.CompilerParams(
            collective_id=0, has_side_effects=True, vmem_limit_bytes=60 * 2**20
        ),
        name="section",
    )(
        query_vectors,
        key_vectors,
        value_vectors,
        prior_state,
        doc_ids,
        norm_gain,
        residual,
        out_weight,
        enc_weight,
        enc_bias,
    )


def solution(mesh):
    sizes = (mesh.shape["section"], mesh.shape["seq"], mesh.shape["head"])
    body = fused if sizes == (2, SEQ, GROUP) else local
    return jax.shard_map(
        body,
        mesh=mesh,
        in_specs=(
            P("section", "seq", "head"),
            P("section", "seq", "head"),
            P("section", "seq", "head"),
            P("section", "head", None, None),
            P("section", "seq"),
            P("section", "head"),
            P("section", "head", "seq"),
            P("section", "head", "seq"),
            P("section", None, ("seq", "head")),
            P("section", ("seq", "head")),
        ),
        out_specs=(P("section", "head", "seq"), P("section", None, ("seq", "head"))),
        check_vma=False,
    )
```

```python
import jax
import jax.numpy as jnp
from jax import lax
from jax.experimental import pallas as pl
from jax.experimental.pallas import tpu as pltpu
from jax.sharding import PartitionSpec as P

HD = 128
POOL = 64
HDIM = 8192


epsilon = 1e-06


def entering(part, axis, combine, identity):
    place = lax.axis_index(axis)
    gathered = jax.tree.map(lambda a: lax.all_gather(a, axis), part)
    state = jax.tree.map(lambda a, e: jnp.zeros_like(a) + jnp.asarray(e, a.dtype), part, identity)

    def one(hop, state):
        return combine(
            state, jax.tree.map(lambda a: lax.dynamic_index_in_dim(a, hop, 0, False), gathered)
        )

    return lax.fori_loop(0, place, one, state)


def passed_along(x, axis, by):
    devices = lax.axis_size(axis)
    return lax.ppermute(x, axis, [(i, (i + by) % devices) for i in range(devices)])


def merge_states(first_pair, second_pair):
    first_state, first_doc = first_pair
    second_state, second_doc = second_pair
    top_doc = jnp.maximum(first_doc, second_doc)
    merged = jnp.where(first_doc == top_doc, first_state, 0.0) + jnp.where(
        second_doc == top_doc, second_state, 0.0
    )
    return (merged, top_doc)


def local(
    query_vectors,
    key_vectors,
    value_vectors,
    prior_state,
    doc_ids,
    norm_gain,
    residual,
    out_weight,
    enc_weight,
    enc_bias,
):
    highest = lax.Precision.HIGHEST
    row_count = query_vectors.shape[1]
    local_heads = query_vectors.shape[2] // HD
    queries = query_vectors[0].reshape(row_count, local_heads, HD)
    keys_block = key_vectors[0].reshape(row_count, local_heads, HD)
    values_block = value_vectors[0].reshape(row_count, local_heads, HD)
    doc_index = doc_ids[0]
    doc_float = doc_index.astype(jnp.float32)
    last_doc = doc_float[-1]
    keys_last = jnp.where(
        (doc_index == doc_index[-1])[:, None, None], keys_block, jnp.zeros_like(keys_block)
    )
    summary = jnp.einsum(
        "thd,the->hde", keys_last, values_block, preferred_element_type=jnp.float32
    )
    identity_pair = (jnp.zeros_like(summary), jnp.full((1,), -1.0, jnp.float32))
    earlier_state, earlier_last = entering(
        (summary, last_doc[None]), "seq", merge_states, identity_pair
    )
    earlier_doc = earlier_last[0]
    incoming_state, incoming_doc = merge_states(
        (prior_state[0], jnp.zeros((), jnp.float32)), (earlier_state, earlier_doc)
    )
    inter = jnp.einsum(
        "thd,hde->the", queries.astype(jnp.float32), incoming_state, precision=highest
    )
    inter = inter * (doc_float == incoming_doc).astype(jnp.float32)[:, None, None]
    scores = jnp.einsum("thd,uhd->htu", queries, keys_block, preferred_element_type=jnp.float32)
    positions = jnp.arange(row_count)
    same_doc = (positions[None, :] <= positions[:, None]) & (
        doc_index[:, None] == doc_index[None, :]
    )
    scores = jnp.where(same_doc[None, :, :], scores, 0.0)
    intra = jnp.einsum("htu,uhe->the", scores, values_block.astype(jnp.float32), precision=highest)
    attended = (inter + intra).reshape(row_count, local_heads * HD)
    total_square = lax.psum(jnp.sum(attended * attended, axis=1), "head")
    inverse_rms = lax.rsqrt(total_square / HDIM + epsilon)
    normed = (attended * inverse_rms[:, None] * norm_gain[0]).astype(jnp.bfloat16)
    projection = out_weight[0]
    partial_sums = jnp.dot(
        lax.all_gather(normed, "seq", axis=0, tiled=True),
        projection,
        preferred_element_type=jnp.float32,
    )
    own_rows = residual[0]
    encoder = enc_weight[0]
    latent_width = encoder.shape[1]
    reduced = lax.psum_scatter(partial_sums, "head", scatter_dimension=0, tiled=True)
    layer_out = (own_rows.astype(jnp.float32) + reduced).astype(jnp.bfloat16)
    features = lax.all_gather(layer_out, "head", axis=0, tiled=True)
    pre_scores = jnp.dot(
        lax.all_gather(features, "seq", axis=1, tiled=True),
        encoder,
        preferred_element_type=jnp.float32,
    )
    latent = jax.nn.relu(pre_scores + enc_bias[0])
    pooled = jnp.mean(latent.reshape(-1, POOL, latent_width), axis=1).astype(jnp.bfloat16)
    handoff, monitor = passed_along((layer_out[None], pooled[None]), "section", 1)
    return (handoff, monitor)


MESH = pl.DeviceIdType.MESH
F32 = jnp.float32
BF16 = jnp.bfloat16
SEQ = 4
GROUP = 4
CHUNKS = 4
HEAD_GROUPS = 8


def fused_kernel(
    q_ref,
    k_ref,
    v_ref,
    prior_ref,
    doc_ref,
    gain_ref,
    res_ref,
    ow_hbm,
    enc_hbm,
    bias_ref,
    hand_ref,
    mon_ref,
    ow,
    enc,
    doc_own,
    doc_prev,
    state_in,
    state_out,
    summary,
    attended,
    sq_own,
    sq_in,
    rows,
    part,
    part_out,
    part_in,
    feats,
    hand_in,
    acc,
    pool,
    pool_in,
    ow_sem,
    enc_sem,
    doc_sem,
    st_s,
    st_r,
    sq_s,
    sq_r,
    row_s,
    row_r,
    part_s,
    part_r,
    zg_s,
    zg_r,
    x_s,
    x_r,
    y_s,
    y_r,
    d_s,
    d_r,
    hand_s,
    hand_r,
    pool_sem,
):
    s = lax.axis_index("section")
    z = lax.axis_index("seq")
    h = lax.axis_index("head")
    tokens = q_ref.shape[1]
    chunk_rows = tokens // CHUNKS
    heads = q_ref.shape[2] // HD
    per_chunk = heads // HEAD_GROUPS
    width = res_ref.shape[2]
    latents = bias_ref.shape[1]
    x_peer = h + 1 - 2 * lax.rem(h, 2)
    y_peer = lax.rem(h + 2, 4)
    d_peer = 3 - h
    mates = (x_peer, y_peer, d_peer)

    def at(seq=None, head=None, section=None):
        return (
            s if section is None else section,
            z if seq is None else seq,
            h if head is None else head,
        )

    def remote(src, dst, send, recv, device):
        return pltpu.make_async_remote_copy(
            src_ref=src, dst_ref=dst, send_sem=send, recv_sem=recv,
            device_id=device, device_id_type=MESH,
        )

    def column(k):
        return lax.rem(z + SEQ - k, SEQ)

    ow_copy = pltpu.make_async_copy(ow_hbm.at[0], ow, ow_sem)
    ow_copy.start()

    def enc_copy(k):
        which = column(k)
        place = pl.ds(pl.multiple_of(which * width, width), width)
        return pltpu.make_async_copy(enc_hbm.at[0, place], enc.at[place], enc_sem.at[k])

    barrier = pltpu.get_barrier_semaphore()
    for k in range(1, SEQ):
        pl.semaphore_signal(barrier, inc=1, device_id=at(seq=lax.rem(z + k, SEQ)), device_id_type=MESH)
    for mate in mates:
        pl.semaphore_signal(barrier, inc=1, device_id=at(head=mate), device_id_type=MESH)
    pl.semaphore_signal(barrier, inc=1, device_id=at(section=1 - s), device_id_type=MESH)
    pl.semaphore_wait(barrier, SEQ - 1 + 3 + 1)

    row_iota = lax.broadcasted_iota(jnp.int32, (tokens, tokens), 0)
    col_iota = lax.broadcasted_iota(jnp.int32, (tokens, tokens), 1)
    eye = row_iota == col_iota
    doc_own[...] = jnp.broadcast_to(doc_ref[...].astype(F32), doc_own.shape)
    later = jnp.minimum(z + 1, SEQ - 1)

    def doc_copy():
        return remote(doc_own, doc_prev, doc_sem.at[0], doc_sem.at[1], at(seq=later))

    def state_copy(c):
        return remote(state_out.at[c], state_in.at[c], st_s.at[c], st_r.at[c], at(seq=later))

    @pl.when(z < SEQ - 1)
    def _():
        doc_copy().start()

    doc_row = doc_own[0:1, :]
    doc_col = jnp.sum(jnp.where(eye, doc_row, 0.0), axis=1, keepdims=True)
    last_doc = jnp.max(doc_row, axis=1, keepdims=True)
    keep_key = doc_col == last_doc
    same_doc = (doc_col == doc_row) & (col_iota <= row_iota)

    def columns(head):
        return slice(head * HD, (head + 1) * HD)

    def summarize(head):
        keys = k_ref[0, :, columns(head)]
        keys = jnp.where(keep_key, keys.astype(F32), 0.0).astype(BF16)
        summary[head] = lax.dot_general(
            keys, v_ref[0, :, columns(head)], (((0,), (0,)), ((), ())), preferred_element_type=F32
        )

    def within(head):
        cols = columns(head)
        values = v_ref[0, :, cols]
        scores = lax.dot_general(
            q_ref[0, :, cols], k_ref[0, :, cols], (((1,), (1,)), ((), ())), preferred_element_type=F32
        )
        scores = jnp.where(same_doc, scores, 0.0)
        high = scores.astype(BF16)
        low = (scores - high.astype(F32)).astype(BF16)
        attended[:, cols] = jnp.dot(high, values, preferred_element_type=F32) + jnp.dot(
            low, values, preferred_element_type=F32
        )

    def send_state(c):
        for i in range(per_chunk):
            head = c * per_chunk + i
            state_out[c, i] = (state_in[c, i].astype(F32) * carried + summary[head]).astype(BF16)
        state_copy(c).start()

    @pl.when(z == 0)
    def _():
        doc_prev[...] = jnp.zeros_like(doc_prev)

    @pl.when(z > 0)
    def _():
        doc_copy().wait_recv()

    entering_doc = jnp.max(doc_prev[0:1, :], axis=1, keepdims=True)
    carried = jnp.where(last_doc == entering_doc, 1.0, 0.0)
    from_before = jnp.where(doc_col == entering_doc, 1.0, 0.0)

    for c in range(HEAD_GROUPS):
        for i in range(per_chunk):
            summarize(c * per_chunk + i)

        @pl.when(z == 0)
        def _():
            state_in[c] = prior_ref[0, c * per_chunk : (c + 1) * per_chunk].astype(BF16)
            send_state(c)

    squares = jnp.zeros((tokens, HD), F32)
    for c in range(HEAD_GROUPS):
        @pl.when(z > 0)
        def _():
            state_copy(c).wait_recv()

        @pl.when((z > 0) & (z < SEQ - 1))
        def _():
            send_state(c)

        for i in range(per_chunk):
            head = c * per_chunk + i
            cols = columns(head)
            within(head)
            inter = jnp.dot(q_ref[0, :, cols], state_in[c, i], preferred_element_type=F32)
            total = attended[:, cols] + inter * from_before
            attended[:, cols] = total
            squares = squares + total * total

    own_sum = jnp.sum(squares, axis=1, keepdims=True)
    sq_own[...] = jnp.broadcast_to(
        jnp.sum(jnp.where(eye, own_sum, 0.0), axis=0, keepdims=True), sq_own.shape
    )

    def sq_copy(i):
        return remote(sq_own, sq_in.at[i], sq_s.at[i], sq_r.at[i], at(head=mates[i]))

    for i in range(3):
        sq_copy(i).start()
    sum_row = sq_own[0:1, :]
    for i in range(3):
        sq_copy(i).wait_recv()
        sum_row = sum_row + sq_in[i, 0:1, :]
    sum_col = jnp.sum(jnp.where(eye, sum_row, 0.0), axis=1, keepdims=True)
    inverse_rms = lax.rsqrt(sum_col / HDIM + epsilon)

    def row_copy(c, k):
        i = c * (SEQ - 1) + k - 1
        return remote(
            rows.at[c, z], rows.at[c, z], row_s.at[i], row_r.at[i], at(seq=lax.rem(z + k, SEQ))
        )

    inner = (z > 0) & (z < SEQ - 1)
    direct = {1: z != SEQ - 1, 2: z >= 0, 3: z != 0}
    relay_target = lax.rem(jnp.maximum(z - 1, 0), 2) * (SEQ - 1)
    relay_sem = lax.rem(2 * z + SEQ - 2, SEQ)
    relay_block = lax.rem(z + 2, SEQ)

    def start_along(copy, c):
        copy(c, 2).start()
        for k in (1, 3):

            @pl.when(direct[k])
            def _():
                copy(c, k).start()

    def wait_along(copy, relayed, c):
        copy(c, 2).wait_recv()

        @pl.when(inner)
        def _():
            relayed(c).start()

        for k in (1, 3):
            copy(c, k).wait_recv()

    def sent_along(copy, relayed, c):
        copy(c, 2).wait_send()
        for k in (1, 3):

            @pl.when(direct[k])
            def _():
                copy(c, k).wait_send()

        @pl.when(inner)
        def _():
            relayed(c).wait_send()

    def row_relay(c):
        block = rows.at[c, relay_block]
        return remote(
            block, block, row_s.at[CHUNKS * (SEQ - 1) + c],
            row_r.at[c * (SEQ - 1) + relay_sem], at(seq=relay_target),
        )

    def z_relay(c):
        block = feats.at[c, relay_block, h]
        return remote(
            block, block, zg_s.at[CHUNKS * (SEQ - 1) + c],
            zg_r.at[c * (SEQ - 1) + relay_sem], at(seq=relay_target),
        )

    def push_rows(c):
        start_along(row_copy, c)

    for c in range(CHUNKS):
        here = slice(c * chunk_rows, (c + 1) * chunk_rows)
        rows[c, z] = (attended[here, :] * inverse_rms[here, :] * gain_ref[...]).astype(BF16)
        if c < 2:
            push_rows(c)

    TILE = 256
    depth = ow.shape[0]

    def project(c):
        wait_along(row_copy, row_relay, c)

        def one(n, carry):
            for u in range(3):
                cols = pl.ds(pl.multiple_of((n * 3 + u) * TILE, TILE), TILE)
                product = jnp.dot(
                    rows[c].reshape(SEQ * chunk_rows, depth), ow[:, cols], preferred_element_type=F32
                ).reshape(GROUP, chunk_rows, TILE)
                part[:, :, cols] = product
                part_out[c, :, :, cols] = product.astype(BF16)
            return carry

        lax.fori_loop(0, width // (3 * TILE), one, 0)
        for i in range(3):
            part_copy(c, i).start()

    def part_copy(c, i):
        j = c * 3 + i
        return remote(
            part_out.at[c, mates[i]], part_in.at[c, i], part_s.at[j], part_r.at[j], at(head=mates[i])
        )

    def z_copy(c, k):
        i = c * (SEQ - 1) + k - 1
        block = feats.at[c, z, h]
        return remote(block, block, zg_s.at[i], zg_r.at[i], at(seq=lax.rem(z + k, SEQ)))

    def hand_copy(c):
        return remote(feats.at[c, z, h], hand_in.at[c], hand_s.at[c], hand_r.at[c], at(section=1 - s))

    def x_copy(c, k):
        i = c * SEQ + k
        block = feats.at[c, column(k), h]
        return remote(block, block, x_s.at[i], x_r.at[i], at(head=x_peer))

    def y_copy(c, k):
        i = c * SEQ + k
        block = feats.at[c, column(k), h]
        return remote(block, block, y_s.at[i], y_r.at[i], at(head=y_peer))

    def d_copy(c, k):
        i = c * SEQ + k
        source, target = (x_peer, y_peer) if k % 2 == 0 else (y_peer, x_peer)
        block = feats.at[c, column(k), source]
        return remote(block, block, d_s.at[i], d_r.at[i], at(head=target))

    def finish(c):
        here = slice(c * chunk_rows, (c + 1) * chunk_rows)
        total = res_ref[0, here, :].astype(F32) + own_part[c]
        for i in range(3):
            part_copy(c, i).wait_recv()
        for i in range(3):
            total = total + part_in[c, i].astype(F32)
        feats[c, z, h] = total.astype(BF16)
        start_along(z_copy, c)
        x_copy(c, 0).start()
        y_copy(c, 0).start()
        hand_copy(c).start()
        if c + 2 < CHUNKS:
            push_rows(c + 2)

    def relay(c):
        wait_along(z_copy, z_relay, c)
        for k in range(1, SEQ):
            x_copy(c, k).start()
            y_copy(c, k).start()

    def forward(c, k):
        (x_copy if k % 2 == 0 else y_copy)(c, k).wait_recv()
        d_copy(c, k).start()

    def encode(p, k):
        for c in (2 * p, 2 * p + 1):
            (y_copy if k % 2 == 0 else x_copy)(c, k).wait_recv()
            d_copy(c, k).wait_recv()
        which = column(k)
        depth_rows = pl.ds(pl.multiple_of(which * width, width), width)
        if p == 0:
            enc_copy(k).wait()

        def one(n, carry):
            for u in range(4):
                cols = pl.ds(pl.multiple_of((n * 4 + u) * TILE, TILE), TILE)
                product = jnp.dot(
                    feats[2 * p : 2 * p + 2, which].reshape(2 * GROUP * chunk_rows, width),
                    enc[depth_rows, cols],
                    preferred_element_type=F32,
                )
                if k == 0:
                    acc[:, cols] = product + bias_ref[:, cols]
                elif k < SEQ - 1:
                    acc[:, cols] += product
                else:
                    latent = jnp.maximum(acc[:, cols] + product, 0.0)
                    latent = latent.reshape(2, GROUP, chunk_rows, TILE)
                    means = jnp.sum(latent[0] + latent[1], axis=1) / POOL
                    for j in range(GROUP):
                        r = j * (tokens // POOL) + p
                        pool[r : r + 1, cols] = means[j : j + 1, :]
            return carry

        lax.fori_loop(0, latents // (4 * TILE), one, 0)

    own_part = {}

    def produce(c):
        project(c)
        enc_copy(c).start()
        own_part[c] = part[h]
        finish(c)

    def pass_on(c):
        for k in range(SEQ):
            forward(c, k)

    ow_copy.wait()
    produce(0)
    produce(1)
    relay(0)
    pass_on(0)
    produce(2)
    relay(1)
    pass_on(1)
    produce(3)
    relay(2)
    pass_on(2)
    encode(0, 0)
    encode(0, 1)
    relay(3)
    encode(0, 2)
    forward(3, 0)
    forward(3, 1)
    encode(0, 3)
    forward(3, 2)
    forward(3, 3)
    for k in range(SEQ):
        encode(1, k)

    pool_copy = remote(pool, pool_in, pool_sem.at[0], pool_sem.at[1], at(section=1 - s))
    pool_copy.start()
    for c in range(CHUNKS):
        hand_copy(c).wait_recv()
        hand_ref[0, c * chunk_rows : (c + 1) * chunk_rows, :] = hand_in[c]
    pool_copy.wait_recv()
    mon_ref[0] = pool_in[...].astype(BF16)

    @pl.when(z < SEQ - 1)
    def _():
        doc_copy().wait_send()
        for c in range(HEAD_GROUPS):
            state_copy(c).wait_send()

    pool_copy.wait_send()
    for i in range(3):
        sq_copy(i).wait_send()
    for c in range(CHUNKS):
        hand_copy(c).wait_send()
        for i in range(3):
            part_copy(c, i).wait_send()
        sent_along(row_copy, row_relay, c)
        sent_along(z_copy, z_relay, c)
        for k in range(SEQ):
            x_copy(c, k).wait_send()
            y_copy(c, k).wait_send()
            d_copy(c, k).wait_send()


def fused(
    query_vectors,
    key_vectors,
    value_vectors,
    prior_state,
    doc_ids,
    norm_gain,
    residual,
    out_weight,
    enc_weight,
    enc_bias,
):
    tokens, features = query_vectors.shape[1:]
    heads = features // HD
    width = residual.shape[2]
    depth, latents = enc_weight.shape[1:]
    chunk_rows = tokens // CHUNKS
    per_chunk = heads // HEAD_GROUPS
    vmem = pl.BlockSpec(memory_space=pltpu.VMEM)
    anywhere = pl.BlockSpec(memory_space=pl.ANY)
    dma = lambda n: pltpu.SemaphoreType.DMA((n,))
    buf = lambda shape, dtype: pltpu.VMEM(shape, dtype)
    return pl.pallas_call(
        fused_kernel,
        out_shape=(
            jax.ShapeDtypeStruct((1, tokens, width), BF16),
            jax.ShapeDtypeStruct((1, SEQ * tokens // POOL, latents), BF16),
        ),
        in_specs=[vmem] * 7 + [anywhere] * 2 + [vmem],
        out_specs=(vmem, vmem),
        scratch_shapes=[
            buf((features, width), BF16),
            buf((depth, latents), BF16),
            buf((8, tokens), F32),
            buf((8, tokens), F32),
            buf((HEAD_GROUPS, per_chunk, HD, HD), BF16),
            buf((HEAD_GROUPS, per_chunk, HD, HD), BF16),
            buf((heads, HD, HD), F32),
            buf((tokens, features), F32),
            buf((8, tokens), F32),
            buf((3, 8, tokens), F32),
            buf((CHUNKS, SEQ, chunk_rows, features), BF16),
            buf((GROUP, chunk_rows, width), F32),
            buf((CHUNKS, GROUP, chunk_rows, width), BF16),
            buf((CHUNKS, 3, chunk_rows, width), BF16),
            buf((CHUNKS, SEQ, GROUP, chunk_rows, width), BF16),
            buf((CHUNKS, chunk_rows, width), BF16),
            buf((2 * GROUP * chunk_rows, latents), F32),
            buf((SEQ * tokens // POOL, latents), F32),
            buf((SEQ * tokens // POOL, latents), F32),
            pltpu.SemaphoreType.DMA,
            dma(SEQ),
            dma(2),
            dma(HEAD_GROUPS),
            dma(HEAD_GROUPS),
            dma(3),
            dma(3),
            dma(CHUNKS * SEQ),
            dma(CHUNKS * (SEQ - 1)),
            dma(CHUNKS * 3),
            dma(CHUNKS * 3),
            dma(CHUNKS * SEQ),
            dma(CHUNKS * (SEQ - 1)),
            dma(CHUNKS * SEQ),
            dma(CHUNKS * SEQ),
            dma(CHUNKS * SEQ),
            dma(CHUNKS * SEQ),
            dma(CHUNKS * SEQ),
            dma(CHUNKS * SEQ),
            dma(CHUNKS),
            dma(CHUNKS),
            dma(2),
        ],
        compiler_params=pltpu.CompilerParams(
            collective_id=0, has_side_effects=True, vmem_limit_bytes=60 * 2**20
        ),
        name="section",
    )(
        query_vectors,
        key_vectors,
        value_vectors,
        prior_state,
        doc_ids,
        norm_gain,
        residual,
        out_weight,
        enc_weight,
        enc_bias,
    )


def solution(mesh):
    sizes = (mesh.shape["section"], mesh.shape["seq"], mesh.shape["head"])
    body = fused if sizes == (2, SEQ, GROUP) else local
    return jax.shard_map(
        body,
        mesh=mesh,
        in_specs=(
            P("section", "seq", "head"),
            P("section", "seq", "head"),
            P("section", "seq", "head"),
            P("section", "head", None, None),
            P("section", "seq"),
            P("section", "head"),
            P("section", "head", "seq"),
            P("section", "head", "seq"),
            P("section", None, ("seq", "head")),
            P("section", ("seq", "head")),
        ),
        out_specs=(P("section", "head", "seq"), P("section", None, ("seq", "head"))),
        check_vma=False,
    )
```
